32 devices in a mesh: grid: 4 (over y, x), row: 4 (over z), rhs: 2 (over core).
Axes of the slice: x: 2, y: 2, z: 4, core: 2. Of those that a mesh axis runs over, the one named last changes fastest.
Arguments:
- leaf_rhs: float32 [12288, 2048], P(('grid', 'row'), 'rhs'), parts along dimension 1, may hold values from -6 to 6
- block_sizes: int32 [16], P(('grid', 'row')), may hold values from 384 to 768, as said below
- leaf_lower: float32 [12288, 256], P(('grid', 'row')), may hold values from -0.25 to 0.25
- leaf_inverse: float32 [12288, 768], P(('grid', 'row')), as said below
- coupling: float32 [8192, 768], P(('grid', 'row')), may hold values from -0.0546875 to 0.0546875
- anc_rows: int32 [8192], P(('grid', 'row')), may hold values from 0 to 767, as said below
- anc_rhs: float32 [768, 2048], P(None, 'rhs'), parts along dimension 1, may hold values from -6 to 6
- anc_inverse: float32 [768, 768], replicated, as said below
Outputs:
- leaf_solution: float32 [12288, 2048], P(('grid', 'row'), 'rhs'), parts along dimension 1
- anc_solution: float32 [768, 2048], P('row', 'rhs'), parts along dimension 1
The draws below stay inside these ranges and needn't reach their ends.
There are 2 independent parts, one for each index of `rhs`. The reference program is written for one: setup_inputs(seed, part) draws one part's arguments, and reference() takes and returns one part's arrays. A program takes and returns all parts, laid end to end along the dimension named above; an argument that names none is the same for every part. Nothing has to cross between parts.
Inputs may be any that keep to these rules, and one draw needn't show every extreme that they name: `block_sizes`: every value lies between 384 and 768; some block row uses all 768 rows and another exactly 384. `anc_rows`: within each block row's 512 entries the ancestor rows are distinct and increasing. `leaf_inverse`: each 768 x 768 block is lower triangular with a unit diagonal. `anc_inverse`: lower triangular with a unit diagonal.
All inputs are finite; a program needn't handle non-finite values.
Results may differ from the reference program's by a relative error of at most 0.0001.
Values sent between devices are 32-bit elements; how exact they have to be, the bound alone decides.
A program may use at most 128 MiB of HBM per device.

```python
import jax
import jax.numpy as jnp
from jax import lax

BS = 768
LR = 256
CR = 512
ANC = 768
NRHS = 1024
NBLK = 16
N_GRID = 4
N_ROW = 4


def unit_lower(key, count, order):
    key_one = jax.random.fold_in(key, 0)
    gauss = jax.random.normal(key_one, (count, order, order), jnp.float32)
    strict = jnp.tril(gauss, -1) * (0.7 / jnp.sqrt(jnp.float32(order)))
    return strict + jnp.eye(order, dtype=jnp.float32)[None]


def draw_leaf_inverse(key, part):
    mine = jax.random.fold_in(key, 11)
    return unit_lower(mine, NBLK, BS).reshape(NBLK * BS, BS)


def draw_anc_inverse(key, part):
    mine = jax.random.fold_in(key, 13)
    return unit_lower(mine, 1, ANC).reshape(ANC, ANC)


def draw_block_sizes(key, part):
    mine = jax.random.fold_in(key, 17)
    key_one, key_two = jax.random.split(mine)
    sizes = jax.random.randint(key_one, (NBLK,), BS // 2, BS + 1, dtype=jnp.int32)
    chosen = jax.random.randint(key_two, (), 0, NBLK, dtype=jnp.int32)
    places = jnp.arange(NBLK, dtype=jnp.int32)
    sizes = jnp.where(places == chosen, BS, sizes)
    sizes = jnp.where(places == (chosen + 1) % NBLK, BS // 2, sizes)
    return sizes.astype(jnp.int32)


def draw_anc_rows(key, part):
    mine = jax.random.fold_in(key, 19)
    keys = jax.random.split(mine, NBLK)

    def pick(single):
        return jnp.sort(jax.random.permutation(single, ANC)[:CR])
    return jax.vmap(pick)(keys).reshape(NBLK * CR).astype(jnp.int32)


def steps_of(stream_key, shape, cuts, low, top_value):
    factor_of, own = 1.0, jax.random.fold_in(stream_key, 6)
    for dim, parts in cuts:
        heights = jnp.exp(jax.random.uniform(jax.random.fold_in(own, dim), (parts,), jnp.float32, low / len(cuts), top_value / len(cuts)))
        factor_of = factor_of * jnp.repeat(heights, shape[dim] // parts).reshape([-1 if axis == dim else 1 for axis in range(len(shape))])
    return factor_of


def noise(stream_key, extent, spread, bound, cuts=(), kind=jnp.bfloat16):
    values = jax.random.normal(stream_key, extent, jnp.float32) * spread
    if len(cuts) > 0:
        values = steps_of(stream_key, extent, cuts, -0.22, 0.18) * values
    return jnp.clip(values, min=-bound, max=bound).astype(kind)


def setup_inputs(seed: int = 0, part: int = 0) -> dict:
    streams_of = jax.random.split(jax.random.key(seed), 9)
    own_keys = jax.random.split(jax.random.fold_in(streams_of[8], part), 9)
    return {
        "leaf_rhs": noise(own_keys[0], (NBLK * BS, NRHS), 1.0, 6.0, ((0, 16),), jnp.float32),
        "block_sizes": draw_block_sizes(jax.random.fold_in(streams_of[8], 71), part),
        "leaf_lower": noise(streams_of[2], (NBLK * BS, LR), (2 * LR) ** -0.5, 0.25, ((0, 16),), jnp.float32),
        "leaf_inverse": draw_leaf_inverse(jax.random.fold_in(streams_of[8], 71), part),
        "coupling": noise(streams_of[4], (NBLK * CR, BS), (BS * NBLK) ** -0.5, 0.0546875, ((0, 16),), jnp.float32),
        "anc_rows": draw_anc_rows(jax.random.fold_in(streams_of[8], 71), part),
        "anc_rhs": noise(own_keys[6], (ANC, NRHS), 1.0, 6.0, (), jnp.float32),
        "anc_inverse": draw_anc_inverse(jax.random.fold_in(streams_of[8], 71), part),
    }


def reference(leaf_rhs, block_sizes, leaf_lower, leaf_inverse, coupling, anc_rows, anc_rhs, anc_inverse):
    highest = lax.Precision.HIGHEST
    blocks_all = N_GRID * N_ROW
    right_blocks = leaf_rhs.reshape(N_GRID, N_ROW, BS, NRHS)
    lower_blocks = leaf_lower.reshape(N_GRID, N_ROW, BS, LR)
    inverses = leaf_inverse.reshape(N_GRID, N_ROW, BS, BS)
    live_rows = (jnp.arange(BS, dtype=jnp.int32)[None, None, :] < block_sizes.reshape(N_GRID, N_ROW)[:, :, None]).astype(jnp.float32)
    carried = jnp.zeros((N_GRID, LR, NRHS), jnp.float32)
    solved_blocks = []
    for level in range(N_ROW):
        reduced = right_blocks[:, level] - jnp.einsum('gbl,gln->gbn', lower_blocks[:, level], carried, precision=highest)
        solved = jnp.einsum('gab,gbn->gan', inverses[:, level], reduced, precision=highest) * live_rows[:, level, :, None]
        solved_blocks.append(solved)
        carried = solved[:, :LR]
    leaf_solution = jnp.stack(solved_blocks, axis=1).reshape(blocks_all * BS, NRHS)
    coupled = jnp.einsum('kcb,kbn->kcn', coupling.reshape(blocks_all, CR, BS), leaf_solution.reshape(blocks_all, BS, NRHS), precision=highest).reshape(blocks_all * CR, NRHS)
    partial_value = jnp.zeros((ANC, NRHS), jnp.float32).at[anc_rows].add(coupled)
    anc_solution = jnp.dot(anc_inverse, anc_rhs - partial_value, precision=highest, preferred_element_type=jnp.float32)
    return leaf_solution, anc_solution
```

```python
import functools

import jax
import jax.numpy as jnp
from jax import lax
from jax.experimental import pallas as pl
from jax.experimental.pallas import tpu as pltpu
from jax.sharding import PartitionSpec as P

MESH = pl.DeviceIdType.MESH
F32 = jnp.float32
BF16 = jnp.bfloat16
CHUNK = 128
TILE = 256


def split(value):
    high = value.astype(BF16)
    return high, (value - high.astype(F32)).astype(BF16)


def dot(left, right):
    return jnp.dot(left, right, preferred_element_type=F32)


def dot_split(left_high, left_low, right_high, right_low):
    small = dot(left_high, right_low) + dot(left_low, right_high)
    return dot(left_high, right_high) + small


def triangle(high_ref, low_ref, tile, right_high, right_low):
    rows = pl.ds(tile * TILE, TILE)
    depth = (tile + 1) * TILE
    return dot_split(
        high_ref[rows, :depth], low_ref[rows, :depth], right_high[:depth], right_low[:depth]
    )


def kernel(
    n_grid, n_row,
    size_ref, rows_ref, rhs_hbm, lower_hbm, inverse_hbm, coupling_hbm, anc_rhs_hbm, anc_inverse_hbm,
    leaf_hbm, anc_ref,
    rhs, lower, inverse, coupling, anc_rhs, anc_inverse,
    inv_high, inv_low, step_high, step_low, onto_high, onto_low, anc_high, anc_low,
    leaf, carried, stage, summed, shares, shares_in, final, final_in,
    load_sem, anc_sem, leaf_sem, chain_send, chain_recv, sum_send, sum_recv,
    share_send, share_recv, final_send, final_recv,
):
    grid, row = lax.axis_index("grid"), lax.axis_index("row")
    block_rows, columns = leaf.shape
    lead = carried.shape[0]
    count = columns // CHUNK
    pairs = count // 2
    owned = count // n_grid
    cycle = n_grid // 2
    share = anc_ref.shape[0]
    tiles = block_rows // TILE
    anc_tiles = anc_high.shape[0] // TILE
    wide = 2 * CHUNK

    def chunk_cols(chunk):
        return pl.ds(pl.multiple_of(chunk * CHUNK, CHUNK), CHUNK)

    def pair_cols(pair):
        return pl.ds(pl.multiple_of(pair * wide, wide), wide)

    def pair_of(turn):
        return (turn // cycle) * cycle + lax.rem(lax.rem(turn, cycle) + grid // 2 + 1, cycle)

    loads = [
        pltpu.make_async_copy(inverse_hbm, inverse, load_sem.at[0]),
        pltpu.make_async_copy(rhs_hbm.at[:lead], rhs.at[:lead], load_sem.at[1]),
        pltpu.make_async_copy(lower_hbm, lower, load_sem.at[2]),
        pltpu.make_async_copy(rhs_hbm.at[lead:], rhs.at[lead:], load_sem.at[3]),
        pltpu.make_async_copy(coupling_hbm, coupling, load_sem.at[4]),
        pltpu.make_async_copy(anc_inverse_hbm, anc_inverse, load_sem.at[5]),
    ]
    for load in loads:
        load.start()
    anc_loads = [
        pltpu.make_async_copy(
            anc_rhs_hbm.at[:, chunk_cols(u * n_grid + grid)], anc_rhs.at[u], anc_sem.at[u]
        )
        for u in range(owned)
    ]
    for load in anc_loads:
        load.start()

    barrier = pltpu.get_barrier_semaphore()
    for off in range(1, n_grid):
        pl.semaphore_signal(
            barrier, inc=1, device_id={"grid": lax.rem(grid + off, n_grid)}, device_id_type=MESH
        )
    for off in range(1, n_row):
        pl.semaphore_signal(
            barrier, inc=1, device_id={"row": lax.rem(row + off, n_row)}, device_id_type=MESH
        )
    pl.semaphore_wait(barrier, n_grid + n_row - 2)

    def chain_copy(chunk):
        return pltpu.make_async_remote_copy(
            src_ref=leaf.at[pl.ds(0, lead), chunk_cols(chunk)],
            dst_ref=carried.at[:, chunk_cols(chunk)],
            send_sem=chain_send.at[chunk],
            recv_sem=chain_recv.at[chunk],
            device_id={"row": lax.rem(row + 1, n_row)},
            device_id_type=MESH,
        )

    def sum_copy(chunk):
        owner = lax.rem(chunk, n_grid)
        off = lax.rem(owner - grid + n_grid, n_grid)
        part = chunk // n_grid
        return off, pltpu.make_async_remote_copy(
            src_ref=stage.at[chunk],
            dst_ref=summed.at[part, off],
            send_sem=sum_send.at[chunk],
            recv_sem=sum_recv.at[part, off],
            device_id={"grid": owner},
            device_id_type=MESH,
        )

    def share_copy(part, off):
        target = lax.rem(row + off, n_row)
        return pltpu.make_async_remote_copy(
            src_ref=shares.at[part, target],
            dst_ref=shares_in.at[part, off],
            send_sem=share_send.at[part, off],
            recv_sem=share_recv.at[part, off],
            device_id={"row": target},
            device_id_type=MESH,
        )

    def final_copy(part, off):
        return pltpu.make_async_remote_copy(
            src_ref=final.at[part],
            dst_ref=final_in.at[part, off],
            send_sem=final_send.at[part, off],
            recv_sem=final_recv.at[part, off],
            device_id={"grid": lax.rem(grid + off, n_grid)},
            device_id_type=MESH,
        )

    def leaf_copy(pair):
        return pltpu.make_async_copy(
            leaf.at[:, pair_cols(pair)], leaf_hbm.at[:, pair_cols(pair)], leaf_sem.at[pair]
        )

    size = size_ref[0]

    def prepare(tile):
        rows = pl.ds(tile * TILE, TILE)
        depth = (tile + 1) * TILE
        place = lax.broadcasted_iota(jnp.int32, (TILE, depth), 0) + tile * TILE
        live = jnp.where(place < size, inverse[rows, :depth], 0.0)
        inv_high[rows, :depth], inv_low[rows, :depth] = split(live)

    loads[0].wait()
    prepare(0)
    loads[1].wait()

    @pl.loop(0, pairs)
    def _(turn):
        pair = pair_of(turn)
        cols = pair_cols(pair)
        high, low = split(rhs[pl.ds(0, TILE), cols])
        leaf[pl.ds(0, TILE), cols] = triangle(inv_high, inv_low, 0, high, low)

        @pl.when(row == 0)
        def _():
            chain_copy(2 * pair).start()
            chain_copy(2 * pair + 1).start()

    for tile in range(1, tiles):
        prepare(tile)
    loads[2].wait()
    lower_high, lower_low = split(lower[...])
    for tile in range(tiles):
        rows = pl.ds(tile * TILE, TILE)
        step = triangle(inv_high, inv_low, tile, lower_high, lower_low)
        step_high[rows, :], step_low[rows, :] = split(step)
    loads[3].wait()

    @pl.loop(0, pairs)
    def _(turn):
        cols = pair_cols(pair_of(turn))
        high, low = split(rhs[:, cols])
        for tile in range(1, tiles):
            leaf[pl.ds(tile * TILE, TILE), cols] = triangle(inv_high, inv_low, tile, high, low)

    loads[4].wait()
    coupling_high, coupling_low = split(coupling[...])
    for tile in range(anc_tiles):
        rows = pl.ds(tile * TILE, TILE)
        place = lax.broadcasted_iota(jnp.int32, (TILE, coupling.shape[0]), 0) + tile * TILE
        chosen = jnp.where(place == rows_ref[...], 1.0, 0.0).astype(BF16)
        onto_high[rows, :] = dot(chosen, coupling_high).astype(BF16)
        onto_low[rows, :] = dot(chosen, coupling_low).astype(BF16)
    loads[5].wait()
    anc_high[...], anc_low[...] = split(anc_inverse[...])

    @pl.loop(0, pairs)
    def _(turn):
        pair = pair_of(turn)
        cols = pair_cols(pair)

        @pl.when(row > 0)
        def _():
            for side in range(2):
                chunk = 2 * pair + side
                chain_copy(chunk).wait_recv()
                high, low = split(carried[:, chunk_cols(chunk)])
                lead_rows = pl.ds(0, TILE)
                leaf[lead_rows, chunk_cols(chunk)] -= dot_split(
                    step_high[lead_rows, :], step_low[lead_rows, :], high, low
                )

                @pl.when(row < n_row - 1)
                def _():
                    chain_copy(chunk).start()

            high, low = split(carried[:, cols])
            for tile in range(1, tiles):
                rows = pl.ds(tile * TILE, TILE)
                leaf[rows, cols] -= dot_split(step_high[rows, :], step_low[rows, :], high, low)

        leaf_copy(pair).start()
        high, low = split(leaf[:, cols])
        for tile in range(anc_tiles):
            rows = pl.ds(tile * TILE, TILE)
            part = dot_split(onto_high[rows, :], onto_low[rows, :], high, low)
            stage[2 * pair, rows, :] = part[:, :CHUNK]
            stage[2 * pair + 1, rows, :] = part[:, CHUNK:]
        for side in range(2):
            off, copy = sum_copy(2 * pair + side)

            @pl.when(off != 0)
            def _():
                copy.start()

    for load in anc_loads:
        load.wait()

    @pl.loop(0, owned)
    def _(part):
        mine = part * n_grid + grid
        for off in range(1, n_grid):
            pltpu.make_async_remote_copy(
                src_ref=stage.at[mine],
                dst_ref=summed.at[part, off],
                send_sem=sum_send.at[mine],
                recv_sem=sum_recv.at[part, off],
                device_id={"grid": lax.rem(grid + off, n_grid)},
                device_id_type=MESH,
            ).wait_recv()
        total = stage[mine] - jnp.where(row == 0, anc_rhs[part], 0.0)
        for off in range(1, n_grid):
            total += summed[part, off]
        high, low = split(total)
        for tile in range(anc_tiles):
            result = triangle(anc_high, anc_low, tile, high, low)
            rows_of(shares, part, tile * TILE, share, result)
        for off in range(1, n_row):
            share_copy(part, off).start()
        own = shares[part, row]
        for off in range(1, n_row):
            share_copy(part, off).wait_recv()
            own += shares_in[part, off]
        final[part] = -own
        for off in range(1, n_grid):
            final_copy(part, off).start()
        anc_ref[:, chunk_cols(mine)] = -own

    @pl.loop(0, owned)
    def _(part):
        for off in range(1, n_grid):
            final_copy(part, off).wait_recv()
            source = part * n_grid + lax.rem(grid - off + n_grid, n_grid)
            anc_ref[:, chunk_cols(source)] = final_in[part, off]
        for off in range(1, n_grid):
            final_copy(part, off).wait_send()
        for off in range(1, n_row):
            share_copy(part, off).wait_send()

    @pl.loop(0, pairs)
    def _(pair):
        leaf_copy(pair).wait()
        for side in range(2):
            chunk = 2 * pair + side

            @pl.when(row < n_row - 1)
            def _():
                chain_copy(chunk).wait_send()

            off, copy = sum_copy(chunk)

            @pl.when(off != 0)
            def _():
                copy.wait_send()


def rows_of(shares, part, first, share, result):
    row, end = first, first + result.shape[0]
    while row < end:
        index, inside = divmod(row, share)
        length = min(share - inside, end - row)
        shares[part, index, inside:inside + length, :] = result[row - first:row - first + length]
        row += length


def body(leaf_rhs, block_sizes, leaf_lower, leaf_inverse, coupling, anc_rows, anc_rhs, anc_inverse):
    n_grid, n_row = lax.axis_size("grid"), lax.axis_size("row")
    block_rows, columns = leaf_rhs.shape
    lead = leaf_lower.shape[1]
    touched = coupling.shape[0]
    anc = anc_inverse.shape[0]
    share = anc // n_row
    count = columns // CHUNK
    owned = count // n_grid
    vmem, dma = pltpu.VMEM, pltpu.SemaphoreType.DMA
    hbm = pl.BlockSpec(memory_space=pl.ANY)
    return pl.pallas_call(
        functools.partial(kernel, n_grid, n_row),
        out_shape=(
            jax.ShapeDtypeStruct((block_rows, columns), F32),
            jax.ShapeDtypeStruct((share, columns), F32),
        ),
        in_specs=[
            pl.BlockSpec(memory_space=pltpu.SMEM),
            pl.BlockSpec(memory_space=pltpu.VMEM),
            hbm, hbm, hbm, hbm, hbm, hbm,
        ],
        out_specs=(hbm, pl.BlockSpec(memory_space=pltpu.VMEM)),
        scratch_shapes=[
            vmem((block_rows, columns), F32),
            vmem((block_rows, lead), F32),
            vmem((block_rows, block_rows), F32),
            vmem((touched, block_rows), F32),
            vmem((owned, anc, CHUNK), F32),
            vmem((anc, anc), F32),
            vmem((block_rows, block_rows), BF16),
            vmem((block_rows, block_rows), BF16),
            vmem((block_rows, lead), BF16),
            vmem((block_rows, lead), BF16),
            vmem((anc, block_rows), BF16),
            vmem((anc, block_rows), BF16),
            vmem((anc, anc), BF16),
            vmem((anc, anc), BF16),
            vmem((block_rows, columns), F32),
            vmem((lead, columns), F32),
            vmem((count, anc, CHUNK), F32),
            vmem((owned, n_grid, anc, CHUNK), F32),
            vmem((owned, n_row, share, CHUNK), F32),
            vmem((owned, n_row, share, CHUNK), F32),
            vmem((owned, share, CHUNK), F32),
            vmem((owned, n_grid, share, CHUNK), F32),
            dma((6,)),
            dma((owned,)),
            dma((count // 2,)),
            dma((count,)),
            dma((count,)),
            dma((count,)),
            dma((owned, n_grid)),
            dma((owned, n_row)),
            dma((owned, n_row)),
            dma((owned, n_grid)),
            dma((owned, n_grid)),
        ],
        compiler_params=pltpu.CompilerParams(
            collective_id=0, has_side_effects=True, vmem_limit_bytes=56 * 1024 * 1024
        ),
        name="forward_solve",
    )(
        block_sizes, anc_rows.reshape(1, touched), leaf_rhs, leaf_lower, leaf_inverse, coupling,
        anc_rhs, anc_inverse,
    )


def solution(mesh):
    placed = (
        P(("grid", "row"), "rhs"),
        P(("grid", "row")),
        P(("grid", "row"), None),
        P(("grid", "row"), None),
        P(("grid", "row"), None),
        P(("grid", "row")),
        P(None, "rhs"),
        P(),
    )
    return jax.shard_map(
        body,
        mesh=mesh,
        in_specs=placed,
        out_specs=(P(("grid", "row"), "rhs"), P("row", "rhs")),
        check_vma=False,
    )
```

```python
import functools

import jax
import jax.numpy as jnp
from jax import lax
from jax.experimental import pallas as pl
from jax.experimental.pallas import tpu as pltpu
from jax.sharding import PartitionSpec as P

MESH = pl.DeviceIdType.MESH
F32 = jnp.float32
BF16 = jnp.bfloat16
CHUNK = 128
TILE = 256


def split(value):
    high = value.astype(BF16)
    return high, (value - high.astype(F32)).astype(BF16)


def dot(left, right):
    return jnp.dot(left, right, preferred_element_type=F32)


def dot_split(left_high, left_low, right_high, right_low):
    small = dot(left_high, right_low) + dot(left_low, right_high)
    return dot(left_high, right_high) + small


def triangle(high_ref, low_ref, tile, right_high, right_low):
    rows = pl.ds(tile * TILE, TILE)
    depth = (tile + 1) * TILE
    return dot_split(
        high_ref[rows, :depth], low_ref[rows, :depth], right_high[:depth], right_low[:depth]
    )


def kernel(
    n_grid, n_row,
    size_ref, rows_ref, rhs_hbm, lower_hbm, inverse_hbm, coupling_hbm, anc_rhs_hbm, anc_inverse_hbm,
    leaf_hbm, anc_ref,
    rhs, lower, inverse, coupling, anc_rhs, anc_inverse,
    coupling_high, coupling_low, inv_high, inv_low, step_high, step_low, onto_high, onto_low, anc_high, anc_low,
    leaf, carried, stage, summed, shares, shares_in, final, final_in,
    load_sem, anc_sem, leaf_sem, chain_send, chain_recv, sum_send, sum_recv,
    share_send, share_recv, final_send, final_recv,
):
    grid, row = lax.axis_index("grid"), lax.axis_index("row")
    block_rows, columns = leaf.shape
    lead = carried.shape[0]
    count = columns // CHUNK
    pairs = count // 2
    owned = count // n_grid
    cycle = n_grid // 2
    share = anc_ref.shape[0]
    tiles = block_rows // TILE
    anc_tiles = anc_high.shape[0] // TILE
    wide = 2 * CHUNK

    def chunk_cols(chunk):
        return pl.ds(pl.multiple_of(chunk * CHUNK, CHUNK), CHUNK)

    def pair_cols(pair):
        return pl.ds(pl.multiple_of(pair * wide, wide), wide)

    def pair_of(turn):
        return (turn // cycle) * cycle + lax.rem(lax.rem(turn, cycle) + grid // 2 + 1, cycle)

    first = [
        pltpu.make_async_copy(
            inverse_hbm.at[:TILE, :TILE], inverse.at[:TILE, :TILE], load_sem.at[0]
        ),
        pltpu.make_async_copy(rhs_hbm.at[:lead], rhs.at[:lead], load_sem.at[1]),
    ]
    loads = [
        pltpu.make_async_copy(lower_hbm, lower, load_sem.at[2]),
        pltpu.make_async_copy(inverse_hbm.at[TILE:], inverse.at[TILE:], load_sem.at[3]),
        pltpu.make_async_copy(rhs_hbm.at[lead:], rhs.at[lead:], load_sem.at[4]),
        pltpu.make_async_copy(coupling_hbm, coupling, load_sem.at[5]),
        pltpu.make_async_copy(anc_inverse_hbm, anc_inverse, load_sem.at[6]),
    ]
    anc_loads = [
        pltpu.make_async_copy(
            anc_rhs_hbm.at[:, chunk_cols(u * n_grid + grid)], anc_rhs.at[u], anc_sem.at[u]
        )
        for u in range(owned)
    ]
    for load in first:
        load.start()

    barrier = pltpu.get_barrier_semaphore()
    for off in range(1, n_grid):
        pl.semaphore_signal(
            barrier, inc=1, device_id={"grid": lax.rem(grid + off, n_grid)}, device_id_type=MESH
        )
    for off in range(1, n_row):
        pl.semaphore_signal(
            barrier, inc=1, device_id={"row": lax.rem(row + off, n_row)}, device_id_type=MESH
        )
    pl.semaphore_wait(barrier, n_grid + n_row - 2)

    def chain_copy(chunk):
        return pltpu.make_async_remote_copy(
            src_ref=leaf.at[pl.ds(0, lead), chunk_cols(chunk)],
            dst_ref=carried.at[:, chunk_cols(chunk)],
            send_sem=chain_send.at[chunk],
            recv_sem=chain_recv.at[chunk],
            device_id={"row": lax.rem(row + 1, n_row)},
            device_id_type=MESH,
        )

    def sum_copy(chunk):
        owner = lax.rem(chunk, n_grid)
        off = lax.rem(owner - grid + n_grid, n_grid)
        part = chunk // n_grid
        return off, pltpu.make_async_remote_copy(
            src_ref=stage.at[chunk],
            dst_ref=summed.at[part, off],
            send_sem=sum_send.at[chunk],
            recv_sem=sum_recv.at[part, off],
            device_id={"grid": owner},
            device_id_type=MESH,
        )

    def share_copy(part, off):
        target = lax.rem(row + off, n_row)
        return pltpu.make_async_remote_copy(
            src_ref=shares.at[part, target],
            dst_ref=shares_in.at[part, off],
            send_sem=share_send.at[part, off],
            recv_sem=share_recv.at[part, off],
            device_id={"row": target},
            device_id_type=MESH,
        )

    def final_copy(part, off):
        return pltpu.make_async_remote_copy(
            src_ref=final.at[part],
            dst_ref=final_in.at[part, off],
            send_sem=final_send.at[part, off],
            recv_sem=final_recv.at[part, off],
            device_id={"grid": lax.rem(grid + off, n_grid)},
            device_id_type=MESH,
        )

    def leaf_copy(pair):
        return pltpu.make_async_copy(
            leaf.at[:, pair_cols(pair)], leaf_hbm.at[:, pair_cols(pair)], leaf_sem.at[pair]
        )

    size = size_ref[0]

    def prepare(tile):
        rows = pl.ds(tile * TILE, TILE)
        depth = (tile + 1) * TILE
        place = lax.broadcasted_iota(jnp.int32, (TILE, depth), 0) + tile * TILE
        live = jnp.where(place < size, inverse[rows, :depth], 0.0)
        inv_high[rows, :depth], inv_low[rows, :depth] = split(live)

    for load in first:
        load.wait()
    for load in loads + anc_loads:
        load.start()
    prepare(0)

    @pl.loop(0, pairs)
    def _(turn):
        pair = pair_of(turn)
        cols = pair_cols(pair)
        high, low = split(rhs[pl.ds(0, TILE), cols])
        leaf[pl.ds(0, TILE), cols] = triangle(inv_high, inv_low, 0, high, low)

        @pl.when(row == 0)
        def _():
            chain_copy(2 * pair).start()
            chain_copy(2 * pair + 1).start()

    loads[0].wait()
    lower_high, lower_low = split(lower[...])
    loads[1].wait()
    for tile in range(tiles):
        if tile > 0:
            prepare(tile)
        rows = pl.ds(tile * TILE, TILE)
        step = triangle(inv_high, inv_low, tile, lower_high, lower_low)
        step_high[rows, :], step_low[rows, :] = split(step)
    for load in loads[2:]:
        load.wait()
    coupling_high[...], coupling_low[...] = split(coupling[...])

    def follow(index):
        chunk = 2 * pair_of(index // 2) + lax.rem(index, 2)
        chain_copy(chunk).wait_recv()
        high, low = split(carried[:, chunk_cols(chunk)])
        lead_rows = pl.ds(0, TILE)
        leaf[lead_rows, chunk_cols(chunk)] -= dot_split(
            step_high[lead_rows, :], step_low[lead_rows, :], high, low
        )

        @pl.when(row < n_row - 1)
        def _():
            chain_copy(chunk).start()

    def rest(turn):
        cols = pair_cols(pair_of(turn))
        high, low = split(rhs[:, cols])
        for tile in range(1, tiles):
            leaf[pl.ds(tile * TILE, TILE), cols] = triangle(inv_high, inv_low, tile, high, low)

    def spread(tile):
        rows = pl.ds(pl.multiple_of(tile * TILE, TILE), TILE)
        place = lax.broadcasted_iota(jnp.int32, (TILE, coupling.shape[0]), 0) + tile * TILE
        chosen = jnp.where(place == rows_ref[...], 1.0, 0.0).astype(BF16)
        onto_high[rows, :] = dot(chosen, coupling_high[...]).astype(BF16)
        onto_low[rows, :] = dot(chosen, coupling_low[...]).astype(BF16)

    def couple(turn):
        pair = pair_of(turn)
        cols = pair_cols(pair)

        @pl.when(row > 0)
        def _():
            high, low = split(carried[:, cols])
            for tile in range(1, tiles):
                rows = pl.ds(tile * TILE, TILE)
                leaf[rows, cols] -= dot_split(step_high[rows, :], step_low[rows, :], high, low)

        leaf_copy(pair).start()
        high, low = split(leaf[:, cols])
        for tile in range(anc_tiles):
            rows = pl.ds(tile * TILE, TILE)
            part = dot_split(onto_high[rows, :], onto_low[rows, :], high, low)
            stage[2 * pair, rows, :] = part[:, :CHUNK]
            stage[2 * pair + 1, rows, :] = part[:, CHUNK:]
        for side in range(2):
            off, copy = sum_copy(2 * pair + side)

            @pl.when(off != 0)
            def _():
                copy.start()

    @pl.loop(0, count + n_row - 2)
    def _(beat):
        index = beat + 1 - row

        @pl.when(jnp.logical_and(row > 0, jnp.logical_and(index >= 0, index < count)))
        def _():
            follow(index)

        @pl.when(beat < anc_tiles)
        def _():
            spread(beat)

        @pl.when(beat < pairs)
        def _():
            rest(beat)

        @pl.when(beat == anc_tiles)
        def _():
            anc_high[...], anc_low[...] = split(anc_inverse[...])

        early = beat - pairs
        is_early = jnp.logical_and(
            jnp.logical_and(early >= 0, early < pairs), early + row <= pairs
        )
        late = (beat + n_row - row) // 2 - n_row // 2
        is_late = jnp.logical_and(
            jnp.logical_and(late >= 0, late < pairs),
            jnp.logical_and(late * 2 + row == beat, late + row > pairs),
        )

        @pl.when(jnp.logical_or(is_early, is_late))
        def _():
            couple(jnp.where(is_early, early, late))

    for load in anc_loads:
        load.wait()

    @pl.loop(0, owned)
    def _(part):
        mine = part * n_grid + grid
        for off in range(1, n_grid):
            pltpu.make_async_remote_copy(
                src_ref=stage.at[mine],
                dst_ref=summed.at[part, off],
                send_sem=sum_send.at[mine],
                recv_sem=sum_recv.at[part, off],
                device_id={"grid": lax.rem(grid + off, n_grid)},
                device_id_type=MESH,
            ).wait_recv()
        total = stage[mine] - jnp.where(row == 0, anc_rhs[part], 0.0)
        for off in range(1, n_grid):
            total += summed[part, off]
        high, low = split(total)
        for tile in range(anc_tiles):
            result = triangle(anc_high, anc_low, tile, high, low)
            rows_of(shares, part, tile * TILE, share, result)
        for off in range(1, n_row):
            share_copy(part, off).start()
        own = shares[part, row]
        for off in range(1, n_row):
            share_copy(part, off).wait_recv()
            own += shares_in[part, off]
        final[part] = -own
        for off in range(1, n_grid):
            final_copy(part, off).start()
        anc_ref[:, chunk_cols(mine)] = -own

    @pl.loop(0, owned)
    def _(part):
        for off in range(1, n_grid):
            final_copy(part, off).wait_recv()
            source = part * n_grid + lax.rem(grid - off + n_grid, n_grid)
            anc_ref[:, chunk_cols(source)] = final_in[part, off]
        for off in range(1, n_grid):
            final_copy(part, off).wait_send()
        for off in range(1, n_row):
            share_copy(part, off).wait_send()

    @pl.loop(0, pairs)
    def _(pair):
        leaf_copy(pair).wait()
        for side in range(2):
            chunk = 2 * pair + side

            @pl.when(row < n_row - 1)
            def _():
                chain_copy(chunk).wait_send()

            off, copy = sum_copy(chunk)

            @pl.when(off != 0)
            def _():
                copy.wait_send()


def rows_of(shares, part, first, share, result):
    row, end = first, first + result.shape[0]
    while row < end:
        index, inside = divmod(row, share)
        length = min(share - inside, end - row)
        shares[part, index, inside:inside + length, :] = result[row - first:row - first + length]
        row += length


def body(leaf_rhs, block_sizes, leaf_lower, leaf_inverse, coupling, anc_rows, anc_rhs, anc_inverse):
    n_grid, n_row = lax.axis_size("grid"), lax.axis_size("row")
    block_rows, columns = leaf_rhs.shape
    lead = leaf_lower.shape[1]
    touched = coupling.shape[0]
    anc = anc_inverse.shape[0]
    share = anc // n_row
    count = columns // CHUNK
    owned = count // n_grid
    vmem, dma = pltpu.VMEM, pltpu.SemaphoreType.DMA
    hbm = pl.BlockSpec(memory_space=pl.ANY)
    return pl.pallas_call(
        functools.partial(kernel, n_grid, n_row),
        out_shape=(
            jax.ShapeDtypeStruct((block_rows, columns), F32),
            jax.ShapeDtypeStruct((share, columns), F32),
        ),
        in_specs=[
            pl.BlockSpec(memory_space=pltpu.SMEM),
            pl.BlockSpec(memory_space=pltpu.VMEM),
            hbm, hbm, hbm, hbm, hbm, hbm,
        ],
        out_specs=(hbm, pl.BlockSpec(memory_space=pltpu.VMEM)),
        scratch_shapes=[
            vmem((block_rows, columns), F32),
            vmem((block_rows, lead), F32),
            vmem((block_rows, block_rows), F32),
            vmem((touched, block_rows), F32),
            vmem((owned, anc, CHUNK), F32),
            vmem((anc, anc), F32),
            vmem((touched, block_rows), BF16),
            vmem((touched, block_rows), BF16),
            vmem((block_rows, block_rows), BF16),
            vmem((block_rows, block_rows), BF16),
            vmem((block_rows, lead), BF16),
            vmem((block_rows, lead), BF16),
            vmem((anc, block_rows), BF16),
            vmem((anc, block_rows), BF16),
            vmem((anc, anc), BF16),
            vmem((anc, anc), BF16),
            vmem((block_rows, columns), F32),
            vmem((lead, columns), F32),
            vmem((count, anc, CHUNK), F32),
            vmem((owned, n_grid, anc, CHUNK), F32),
            vmem((owned, n_row, share, CHUNK), F32),
            vmem((owned, n_row, share, CHUNK), F32),
            vmem((owned, share, CHUNK), F32),
            vmem((owned, n_grid, share, CHUNK), F32),
            dma((7,)),
            dma((owned,)),
            dma((count // 2,)),
            dma((count,)),
            dma((count,)),
            dma((count,)),
            dma((owned, n_grid)),
            dma((owned, n_row)),
            dma((owned, n_row)),
            dma((owned, n_grid)),
            dma((owned, n_grid)),
        ],
        compiler_params=pltpu.CompilerParams(
            collective_id=0, has_side_effects=True, vmem_limit_bytes=56 * 1024 * 1024
        ),
        name="forward_solve",
    )(
        block_sizes, anc_rows.reshape(1, touched), leaf_rhs, leaf_lower, leaf_inverse, coupling,
        anc_rhs, anc_inverse,
    )


def solution(mesh):
    placed = (
        P(("grid", "row"), "rhs"),
        P(("grid", "row")),
        P(("grid", "row"), None),
        P(("grid", "row"), None),
        P(("grid", "row"), None),
        P(("grid", "row")),
        P(None, "rhs"),
        P(),
    )
    return jax.shard_map(
        body,
        mesh=mesh,
        in_specs=placed,
        out_specs=(P(("grid", "row"), "rhs"), P("row", "rhs")),
        check_vma=False,
    )
```

```python
import functools

import jax
import jax.numpy as jnp
from jax import lax
from jax.experimental import pallas as pl
from jax.experimental.pallas import tpu as pltpu
from jax.sharding import PartitionSpec as P

MESH = pl.DeviceIdType.MESH
F32 = jnp.float32
BF16 = jnp.bfloat16
CHUNK = 128
TILE = 256


def split(value):
    high = value.astype(BF16)
    return high, (value - high.astype(F32)).astype(BF16)


def dot(left, right):
    return jnp.dot(left, right, preferred_element_type=F32)


def dot_split(left_high, left_low, right_high, right_low):
    small = dot(left_high, right_low) + dot(left_low, right_high)
    return dot(left_high, right_high) + small


def triangle(high_ref, low_ref, tile, right_high, right_low):
    rows = pl.ds(tile * TILE, TILE)
    depth = (tile + 1) * TILE
    return dot_split(
        high_ref[rows, :depth], low_ref[rows, :depth], right_high[:depth], right_low[:depth]
    )


def kernel(
    n_grid, n_row,
    size_ref, rows_ref, rhs_hbm, lower_hbm, inverse_hbm, coupling_hbm, anc_rhs_hbm, anc_inverse_hbm,
    leaf_hbm, anc_ref,
    rhs, lower, inverse, coupling, anc_rhs, anc_inverse,
    inv_high, inv_low, step_high, step_low, onto_high, onto_low, anc_high, anc_low,
    leaf, carried, stage, summed, shares, shares_in, final, final_in,
    load_sem, anc_sem, leaf_sem, chain_send, chain_recv, sum_send, sum_recv,
    share_send, share_recv, final_send, final_recv,
):
    grid, row = lax.axis_index("grid"), lax.axis_index("row")
    block_rows, columns = leaf.shape
    lead = carried.shape[0]
    count = columns // CHUNK
    pairs = count // 2
    owned = count // n_grid
    cycle = n_grid // 2
    share = anc_ref.shape[0]
    tiles = block_rows // TILE
    anc_tiles = anc_high.shape[0] // TILE
    wide = 2 * CHUNK

    def chunk_cols(chunk):
        return pl.ds(pl.multiple_of(chunk * CHUNK, CHUNK), CHUNK)

    def pair_cols(pair):
        return pl.ds(pl.multiple_of(pair * wide, wide), wide)

    def pair_of(turn):
        return (turn // cycle) * cycle + lax.rem(lax.rem(turn, cycle) + grid // 2 + 1, cycle)

    loads = [
        pltpu.make_async_copy(inverse_hbm, inverse, load_sem.at[0]),
        pltpu.make_async_copy(rhs_hbm.at[:lead], rhs.at[:lead], load_sem.at[1]),
        pltpu.make_async_copy(lower_hbm, lower, load_sem.at[2]),
        pltpu.make_async_copy(rhs_hbm.at[lead:], rhs.at[lead:], load_sem.at[3]),
        pltpu.make_async_copy(coupling_hbm, coupling, load_sem.at[4]),
        pltpu.make_async_copy(anc_inverse_hbm, anc_inverse, load_sem.at[5]),
    ]
    for load in loads:
        load.start()
    anc_loads = [
        pltpu.make_async_copy(
            anc_rhs_hbm.at[:, chunk_cols(u * n_grid + grid)], anc_rhs.at[u], anc_sem.at[u]
        )
        for u in range(owned)
    ]
    for load in anc_loads:
        load.start()

    barrier = pltpu.get_barrier_semaphore()
    for off in range(1, n_grid):
        pl.semaphore_signal(
            barrier, inc=1, device_id={"grid": lax.rem(grid + off, n_grid)}, device_id_type=MESH
        )
    for off in range(1, n_row):
        pl.semaphore_signal(
            barrier, inc=1, device_id={"row": lax.rem(row + off, n_row)}, device_id_type=MESH
        )
    pl.semaphore_wait(barrier, n_grid + n_row - 2)

    def chain_copy(chunk):
        return pltpu.make_async_remote_copy(
            src_ref=leaf.at[pl.ds(0, lead), chunk_cols(chunk)],
            dst_ref=carried.at[:, chunk_cols(chunk)],
            send_sem=chain_send.at[chunk],
            recv_sem=chain_recv.at[chunk],
            device_id={"row": lax.rem(row + 1, n_row)},
            device_id_type=MESH,
        )

    def sum_copy(chunk):
        owner = lax.rem(chunk, n_grid)
        off = lax.rem(owner - grid + n_grid, n_grid)
        part = chunk // n_grid
        return off, pltpu.make_async_remote_copy(
            src_ref=stage.at[chunk],
            dst_ref=summed.at[part, off],
            send_sem=sum_send.at[chunk],
            recv_sem=sum_recv.at[part, off],
            device_id={"grid": owner},
            device_id_type=MESH,
        )

    def share_copy(part, off):
        target = lax.rem(row + off, n_row)
        return pltpu.make_async_remote_copy(
            src_ref=shares.at[part, target],
            dst_ref=shares_in.at[part, off],
            send_sem=share_send.at[part, off],
            recv_sem=share_recv.at[part, off],
            device_id={"row": target},
            device_id_type=MESH,
        )

    def final_copy(part, off):
        return pltpu.make_async_remote_copy(
            src_ref=final.at[part],
            dst_ref=final_in.at[part, off],
            send_sem=final_send.at[part, off],
            recv_sem=final_recv.at[part, off],
            device_id={"grid": lax.rem(grid + off, n_grid)},
            device_id_type=MESH,
        )

    def leaf_copy(pair):
        return pltpu.make_async_copy(
            leaf.at[:, pair_cols(pair)], leaf_hbm.at[:, pair_cols(pair)], leaf_sem.at[pair]
        )

    size = size_ref[0]

    def prepare(tile):
        rows = pl.ds(tile * TILE, TILE)
        depth = (tile + 1) * TILE
        place = lax.broadcasted_iota(jnp.int32, (TILE, depth), 0) + tile * TILE
        live = jnp.where(place < size, inverse[rows, :depth], 0.0)
        inv_high[rows, :depth], inv_low[rows, :depth] = split(live)

    def send_on(turn):
        @pl.when(jnp.logical_and(row == 0, turn < pairs))
        def _():
            pair = pair_of(turn)
            chain_copy(2 * pair).start()
            chain_copy(2 * pair + 1).start()

    loads[0].wait()
    prepare(0)
    loads[1].wait()

    @pl.loop(0, pairs)
    def _(turn):
        pair = pair_of(turn)
        cols = pair_cols(pair)
        high, low = split(rhs[pl.ds(0, TILE), cols])
        leaf[pl.ds(0, TILE), cols] = triangle(inv_high, inv_low, 0, high, low)

        @pl.when(turn == 0)
        def _():
            send_on(0)

    for tile in range(1, tiles):
        prepare(tile)
    loads[2].wait()
    lower_high, lower_low = split(lower[...])
    for tile in range(tiles):
        rows = pl.ds(tile * TILE, TILE)
        step = triangle(inv_high, inv_low, tile, lower_high, lower_low)
        step_high[rows, :], step_low[rows, :] = split(step)
    loads[3].wait()

    send_on(1)

    @pl.loop(0, pairs)
    def _(turn):
        cols = pair_cols(pair_of(turn))
        high, low = split(rhs[:, cols])
        for tile in range(1, tiles):
            leaf[pl.ds(tile * TILE, TILE), cols] = triangle(inv_high, inv_low, tile, high, low)

    loads[4].wait()
    coupling_high, coupling_low = split(coupling[...])
    for tile in range(anc_tiles):
        rows = pl.ds(tile * TILE, TILE)
        place = lax.broadcasted_iota(jnp.int32, (TILE, coupling.shape[0]), 0) + tile * TILE
        chosen = jnp.where(place == rows_ref[...], 1.0, 0.0).astype(BF16)
        onto_high[rows, :] = dot(chosen, coupling_high).astype(BF16)
        onto_low[rows, :] = dot(chosen, coupling_low).astype(BF16)
    loads[5].wait()
    anc_high[...], anc_low[...] = split(anc_inverse[...])

    @pl.loop(0, pairs)
    def _(turn):
        pair = pair_of(turn)
        cols = pair_cols(pair)

        @pl.when(row > 0)
        def _():
            for side in range(2):
                chunk = 2 * pair + side
                chain_copy(chunk).wait_recv()
                high, low = split(carried[:, chunk_cols(chunk)])
                lead_rows = pl.ds(0, TILE)
                leaf[lead_rows, chunk_cols(chunk)] -= dot_split(
                    step_high[lead_rows, :], step_low[lead_rows, :], high, low
                )

                @pl.when(row < n_row - 1)
                def _():
                    chain_copy(chunk).start()

            high, low = split(carried[:, cols])
            for tile in range(1, tiles):
                rows = pl.ds(tile * TILE, TILE)
                leaf[rows, cols] -= dot_split(step_high[rows, :], step_low[rows, :], high, low)

        send_on(turn + 2)
        leaf_copy(pair).start()
        high, low = split(leaf[:, cols])
        for tile in range(anc_tiles):
            rows = pl.ds(tile * TILE, TILE)
            part = dot_split(onto_high[rows, :], onto_low[rows, :], high, low)
            stage[2 * pair, rows, :] = part[:, :CHUNK]
            stage[2 * pair + 1, rows, :] = part[:, CHUNK:]
        for side in range(2):
            off, copy = sum_copy(2 * pair + side)

            @pl.when(off != 0)
            def _():
                copy.start()

    for load in anc_loads:
        load.wait()

    @pl.loop(0, owned)
    def _(part):
        mine = part * n_grid + grid
        for off in range(1, n_grid):
            pltpu.make_async_remote_copy(
                src_ref=stage.at[mine],
                dst_ref=summed.at[part, off],
                send_sem=sum_send.at[mine],
                recv_sem=sum_recv.at[part, off],
                device_id={"grid": lax.rem(grid + off, n_grid)},
                device_id_type=MESH,
            ).wait_recv()
        total = stage[mine] - jnp.where(row == 0, anc_rhs[part], 0.0)
        for off in range(1, n_grid):
            total += summed[part, off]
        high, low = split(total)
        for tile in range(anc_tiles):
            result = triangle(anc_high, anc_low, tile, high, low)
            rows_of(shares, part, tile * TILE, share, result)
        for off in range(1, n_row):
            share_copy(part, off).start()

    @pl.loop(0, owned)
    def _(part):
        mine = part * n_grid + grid
        own = shares[part, row]
        for off in range(1, n_row):
            share_copy(part, off).wait_recv()
            own += shares_in[part, off]
        final[part] = -own
        for off in range(1, n_grid):
            final_copy(part, off).start()
        anc_ref[:, chunk_cols(mine)] = -own

    @pl.loop(0, owned)
    def _(part):
        for off in range(1, n_grid):
            final_copy(part, off).wait_recv()
            source = part * n_grid + lax.rem(grid - off + n_grid, n_grid)
            anc_ref[:, chunk_cols(source)] = final_in[part, off]
        for off in range(1, n_grid):
            final_copy(part, off).wait_send()
        for off in range(1, n_row):
            share_copy(part, off).wait_send()

    @pl.loop(0, pairs)
    def _(pair):
        leaf_copy(pair).wait()
        for side in range(2):
            chunk = 2 * pair + side

            @pl.when(row < n_row - 1)
            def _():
                chain_copy(chunk).wait_send()

            off, copy = sum_copy(chunk)

            @pl.when(off != 0)
            def _():
                copy.wait_send()


def rows_of(shares, part, first, share, result):
    row, end = first, first + result.shape[0]
    while row < end:
        index, inside = divmod(row, share)
        length = min(share - inside, end - row)
        shares[part, index, inside:inside + length, :] = result[row - first:row - first + length]
        row += length


def body(leaf_rhs, block_sizes, leaf_lower, leaf_inverse, coupling, anc_rows, anc_rhs, anc_inverse):
    n_grid, n_row = lax.axis_size("grid"), lax.axis_size("row")
    block_rows, columns = leaf_rhs.shape
    lead = leaf_lower.shape[1]
    touched = coupling.shape[0]
    anc = anc_inverse.shape[0]
    share = anc // n_row
    count = columns // CHUNK
    owned = count // n_grid
    vmem, dma = pltpu.VMEM, pltpu.SemaphoreType.DMA
    hbm = pl.BlockSpec(memory_space=pl.ANY)
    return pl.pallas_call(
        functools.partial(kernel, n_grid, n_row),
        out_shape=(
            jax.ShapeDtypeStruct((block_rows, columns), F32),
            jax.ShapeDtypeStruct((share, columns), F32),
        ),
        in_specs=[
            pl.BlockSpec(memory_space=pltpu.SMEM),
            pl.BlockSpec(memory_space=pltpu.VMEM),
            hbm, hbm, hbm, hbm, hbm, hbm,
        ],
        out_specs=(hbm, pl.BlockSpec(memory_space=pltpu.VMEM)),
        scratch_shapes=[
            vmem((block_rows, columns), F32),
            vmem((block_rows, lead), F32),
            vmem((block_rows, block_rows), F32),
            vmem((touched, block_rows), F32),
            vmem((owned, anc, CHUNK), F32),
            vmem((anc, anc), F32),
            vmem((block_rows, block_rows), BF16),
            vmem((block_rows, block_rows), BF16),
            vmem((block_rows, lead), BF16),
            vmem((block_rows, lead), BF16),
            vmem((anc, block_rows), BF16),
            vmem((anc, block_rows), BF16),
            vmem((anc, anc), BF16),
            vmem((anc, anc), BF16),
            vmem((block_rows, columns), F32),
            vmem((lead, columns), F32),
            vmem((count, anc, CHUNK), F32),
            vmem((owned, n_grid, anc, CHUNK), F32),
            vmem((owned, n_row, share, CHUNK), F32),
            vmem((owned, n_row, share, CHUNK), F32),
            vmem((owned, share, CHUNK), F32),
            vmem((owned, n_grid, share, CHUNK), F32),
            dma((6,)),
            dma((owned,)),
            dma((count // 2,)),
            dma((count,)),
            dma((count,)),
            dma((count,)),
            dma((owned, n_grid)),
            dma((owned, n_row)),
            dma((owned, n_row)),
            dma((owned, n_grid)),
            dma((owned, n_grid)),
        ],
        compiler_params=pltpu.CompilerParams(
            collective_id=0, has_side_effects=True, vmem_limit_bytes=56 * 1024 * 1024
        ),
        name="forward_solve",
    )(
        block_sizes, anc_rows.reshape(1, touched), leaf_rhs, leaf_lower, leaf_inverse, coupling,
        anc_rhs, anc_inverse,
    )


def solution(mesh):
    placed = (
        P(("grid", "row"), "rhs"),
        P(("grid", "row")),
        P(("grid", "row"), None),
        P(("grid", "row"), None),
        P(("grid", "row"), None),
        P(("grid", "row")),
        P(None, "rhs"),
        P(),
    )
    return jax.shard_map(
        body,
        mesh=mesh,
        in_specs=placed,
        out_specs=(P(("grid", "row"), "rhs"), P("row", "rhs")),
        check_vma=False,
    )
```

```python
import functools

import jax
import jax.numpy as jnp
from jax import lax
from jax.experimental import pallas as pl
from jax.experimental.pallas import tpu as pltpu
from jax.sharding import PartitionSpec as P

MESH = pl.DeviceIdType.MESH
F32 = jnp.float32
BF16 = jnp.bfloat16
CHUNK = 128
TILE = 256


def split(value):
    high = value.astype(BF16)
    return high, (value - high.astype(F32)).astype(BF16)


def dot(left, right):
    return jnp.dot(left, right, preferred_element_type=F32)


def dot_split(left_high, left_low, right_high, right_low):
    small = dot(left_high, right_low) + dot(left_low, right_high)
    return dot(left_high, right_high) + small


def triangle(high_ref, low_ref, tile, right_high, right_low):
    rows = pl.ds(tile * TILE, TILE)
    depth = (tile + 1) * TILE
    return dot_split(
        high_ref[rows, :depth], low_ref[rows, :depth], right_high[:depth], right_low[:depth]
    )


def kernel(
    n_grid, n_row,
    size_ref, rows_ref, rhs_hbm, lower_hbm, inverse_hbm, coupling_hbm, anc_rhs_hbm, anc_inverse_hbm,
    leaf_hbm, anc_ref,
    rhs, lower, inverse, coupling, anc_rhs, anc_inverse,
    inv_high, inv_low, step_high, step_low, onto_high, onto_low, anc_high, anc_low,
    leaf, carried, stage, summed, shares, shares_in, final, final_in,
    load_sem, anc_sem, leaf_sem, chain_send, chain_recv, sum_send, sum_recv,
    share_send, share_recv, final_send, final_recv,
):
    grid, row = lax.axis_index("grid"), lax.axis_index("row")
    block_rows, columns = leaf.shape
    lead = carried.shape[0]
    count = columns // CHUNK
    pairs = count // 2
    owned = count // n_grid
    cycle = n_grid // 2
    share = anc_ref.shape[0]
    tiles = block_rows // TILE
    anc_tiles = anc_high.shape[0] // TILE
    wide = 2 * CHUNK

    def chunk_cols(chunk):
        return pl.ds(pl.multiple_of(chunk * CHUNK, CHUNK), CHUNK)

    def pair_cols(pair):
        return pl.ds(pl.multiple_of(pair * wide, wide), wide)

    def pair_of(turn):
        return lax.rem(turn, owned) * cycle + lax.rem(turn // owned + grid // 2 + 1, cycle)

    loads = [
        pltpu.make_async_copy(inverse_hbm, inverse, load_sem.at[0]),
        pltpu.make_async_copy(rhs_hbm.at[:lead], rhs.at[:lead], load_sem.at[1]),
        pltpu.make_async_copy(lower_hbm, lower, load_sem.at[2]),
        pltpu.make_async_copy(rhs_hbm.at[lead:], rhs.at[lead:], load_sem.at[3]),
        pltpu.make_async_copy(coupling_hbm, coupling, load_sem.at[4]),
        pltpu.make_async_copy(anc_inverse_hbm, anc_inverse, load_sem.at[5]),
    ]
    for load in loads:
        load.start()
    anc_loads = [
        pltpu.make_async_copy(
            anc_rhs_hbm.at[:, chunk_cols(u * n_grid + grid)], anc_rhs.at[u], anc_sem.at[u]
        )
        for u in range(owned)
    ]
    for load in anc_loads:
        load.start()

    barrier = pltpu.get_barrier_semaphore()
    for off in range(1, n_grid):
        pl.semaphore_signal(
            barrier, inc=1, device_id={"grid": lax.rem(grid + off, n_grid)}, device_id_type=MESH
        )
    for off in range(1, n_row):
        pl.semaphore_signal(
            barrier, inc=1, device_id={"row": lax.rem(row + off, n_row)}, device_id_type=MESH
        )
    pl.semaphore_wait(barrier, n_grid + n_row - 2)

    def chain_copy(chunk):
        return pltpu.make_async_remote_copy(
            src_ref=leaf.at[pl.ds(0, lead), chunk_cols(chunk)],
            dst_ref=carried.at[:, chunk_cols(chunk)],
            send_sem=chain_send.at[chunk],
            recv_sem=chain_recv.at[chunk],
            device_id={"row": lax.rem(row + 1, n_row)},
            device_id_type=MESH,
        )

    def sum_copy(chunk):
        owner = lax.rem(chunk, n_grid)
        off = lax.rem(owner - grid + n_grid, n_grid)
        part = chunk // n_grid
        return off, pltpu.make_async_remote_copy(
            src_ref=stage.at[chunk],
            dst_ref=summed.at[part, off],
            send_sem=sum_send.at[chunk],
            recv_sem=sum_recv.at[part, off],
            device_id={"grid": owner},
            device_id_type=MESH,
        )

    def share_copy(part, off):
        target = lax.rem(row + off, n_row)
        return pltpu.make_async_remote_copy(
            src_ref=shares.at[part, target],
            dst_ref=shares_in.at[part, off],
            send_sem=share_send.at[part, off],
            recv_sem=share_recv.at[part, off],
            device_id={"row": target},
            device_id_type=MESH,
        )

    def final_copy(part, off):
        return pltpu.make_async_remote_copy(
            src_ref=final.at[part],
            dst_ref=final_in.at[part, off],
            send_sem=final_send.at[part, off],
            recv_sem=final_recv.at[part, off],
            device_id={"grid": lax.rem(grid + off, n_grid)},
            device_id_type=MESH,
        )

    def leaf_copy(pair):
        return pltpu.make_async_copy(
            leaf.at[:, pair_cols(pair)], leaf_hbm.at[:, pair_cols(pair)], leaf_sem.at[pair]
        )

    size = size_ref[0]

    def prepare(tile):
        rows = pl.ds(tile * TILE, TILE)
        depth = (tile + 1) * TILE
        place = lax.broadcasted_iota(jnp.int32, (TILE, depth), 0) + tile * TILE
        live = jnp.where(place < size, inverse[rows, :depth], 0.0)
        inv_high[rows, :depth], inv_low[rows, :depth] = split(live)

    def send_on(turn):
        @pl.when(jnp.logical_and(row == 0, turn < pairs))
        def _():
            pair = pair_of(turn)
            chain_copy(2 * pair).start()
            chain_copy(2 * pair + 1).start()

    loads[0].wait()
    prepare(0)
    loads[1].wait()

    @pl.loop(0, pairs)
    def _(turn):
        pair = pair_of(turn)
        cols = pair_cols(pair)
        high, low = split(rhs[pl.ds(0, TILE), cols])
        leaf[pl.ds(0, TILE), cols] = triangle(inv_high, inv_low, 0, high, low)

        @pl.when(turn == 0)
        def _():
            send_on(0)

    for tile in range(1, tiles):
        prepare(tile)
    loads[2].wait()
    lower_high, lower_low = split(lower[...])
    for tile in range(tiles):
        rows = pl.ds(tile * TILE, TILE)
        step = triangle(inv_high, inv_low, tile, lower_high, lower_low)
        step_high[rows, :], step_low[rows, :] = split(step)
    loads[3].wait()

    send_on(1)

    @pl.loop(0, pairs)
    def _(turn):
        cols = pair_cols(pair_of(turn))
        high, low = split(rhs[:, cols])
        for tile in range(1, tiles):
            leaf[pl.ds(tile * TILE, TILE), cols] = triangle(inv_high, inv_low, tile, high, low)

    loads[4].wait()
    coupling_high, coupling_low = split(coupling[...])
    for tile in range(anc_tiles):
        rows = pl.ds(tile * TILE, TILE)
        place = lax.broadcasted_iota(jnp.int32, (TILE, coupling.shape[0]), 0) + tile * TILE
        chosen = jnp.where(place == rows_ref[...], 1.0, 0.0).astype(BF16)
        onto_high[rows, :] = dot(chosen, coupling_high).astype(BF16)
        onto_low[rows, :] = dot(chosen, coupling_low).astype(BF16)
    loads[5].wait()
    anc_high[...], anc_low[...] = split(anc_inverse[...])

    @pl.loop(0, pairs)
    def _(turn):
        pair = pair_of(turn)
        cols = pair_cols(pair)

        @pl.when(row > 0)
        def _():
            for side in range(2):
                chunk = 2 * pair + side
                chain_copy(chunk).wait_recv()
                high, low = split(carried[:, chunk_cols(chunk)])
                lead_rows = pl.ds(0, TILE)
                leaf[lead_rows, chunk_cols(chunk)] -= dot_split(
                    step_high[lead_rows, :], step_low[lead_rows, :], high, low
                )

                @pl.when(row < n_row - 1)
                def _():
                    chain_copy(chunk).start()

            high, low = split(carried[:, cols])
            for tile in range(1, tiles):
                rows = pl.ds(tile * TILE, TILE)
                leaf[rows, cols] -= dot_split(step_high[rows, :], step_low[rows, :], high, low)

        send_on(turn + 2)
        leaf_copy(pair).start()
        high, low = split(leaf[:, cols])
        for tile in range(anc_tiles):
            rows = pl.ds(tile * TILE, TILE)
            part = dot_split(onto_high[rows, :], onto_low[rows, :], high, low)
            stage[2 * pair, rows, :] = part[:, :CHUNK]
            stage[2 * pair + 1, rows, :] = part[:, CHUNK:]
        for side in range(2):
            off, copy = sum_copy(2 * pair + side)

            @pl.when(off != 0)
            def _():
                copy.start()

    for load in anc_loads:
        load.wait()

    @pl.loop(0, owned)
    def _(part):
        mine = part * n_grid + grid
        for off in range(1, n_grid):
            pltpu.make_async_remote_copy(
                src_ref=stage.at[mine],
                dst_ref=summed.at[part, off],
                send_sem=sum_send.at[mine],
                recv_sem=sum_recv.at[part, off],
                device_id={"grid": lax.rem(grid + off, n_grid)},
                device_id_type=MESH,
            ).wait_recv()
        total = stage[mine] - jnp.where(row == 0, anc_rhs[part], 0.0)
        for off in range(1, n_grid):
            total += summed[part, off]
        high, low = split(total)
        for tile in range(anc_tiles):
            result = triangle(anc_high, anc_low, tile, high, low)
            rows_of(shares, part, tile * TILE, share, result)
        for off in range(1, n_row):
            share_copy(part, off).start()

    @pl.loop(0, owned)
    def _(part):
        mine = part * n_grid + grid
        own = shares[part, row]
        for off in range(1, n_row):
            share_copy(part, off).wait_recv()
            own += shares_in[part, off]
        final[part] = -own
        for off in range(1, n_grid):
            final_copy(part, off).start()
        anc_ref[:, chunk_cols(mine)] = -own

    @pl.loop(0, owned)
    def _(part):
        for off in range(1, n_grid):
            final_copy(part, off).wait_recv()
            source = part * n_grid + lax.rem(grid - off + n_grid, n_grid)
            anc_ref[:, chunk_cols(source)] = final_in[part, off]
        for off in range(1, n_grid):
            final_copy(part, off).wait_send()
        for off in range(1, n_row):
            share_copy(part, off).wait_send()

    @pl.loop(0, pairs)
    def _(pair):
        leaf_copy(pair).wait()
        for side in range(2):
            chunk = 2 * pair + side

            @pl.when(row < n_row - 1)
            def _():
                chain_copy(chunk).wait_send()

            off, copy = sum_copy(chunk)

            @pl.when(off != 0)
            def _():
                copy.wait_send()


def rows_of(shares, part, first, share, result):
    row, end = first, first + result.shape[0]
    while row < end:
        index, inside = divmod(row, share)
        length = min(share - inside, end - row)
        shares[part, index, inside:inside + length, :] = result[row - first:row - first + length]
        row += length


def body(leaf_rhs, block_sizes, leaf_lower, leaf_inverse, coupling, anc_rows, anc_rhs, anc_inverse):
    n_grid, n_row = lax.axis_size("grid"), lax.axis_size("row")
    block_rows, columns = leaf_rhs.shape
    lead = leaf_lower.shape[1]
    touched = coupling.shape[0]
    anc = anc_inverse.shape[0]
    share = anc // n_row
    count = columns // CHUNK
    owned = count // n_grid
    vmem, dma = pltpu.VMEM, pltpu.SemaphoreType.DMA
    hbm = pl.BlockSpec(memory_space=pl.ANY)
    return pl.pallas_call(
        functools.partial(kernel, n_grid, n_row),
        out_shape=(
            jax.ShapeDtypeStruct((block_rows, columns), F32),
            jax.ShapeDtypeStruct((share, columns), F32),
        ),
        in_specs=[
            pl.BlockSpec(memory_space=pltpu.SMEM),
            pl.BlockSpec(memory_space=pltpu.VMEM),
            hbm, hbm, hbm, hbm, hbm, hbm,
        ],
        out_specs=(hbm, pl.BlockSpec(memory_space=pltpu.VMEM)),
        scratch_shapes=[
            vmem((block_rows, columns), F32),
            vmem((block_rows, lead), F32),
            vmem((block_rows, block_rows), F32),
            vmem((touched, block_rows), F32),
            vmem((owned, anc, CHUNK), F32),
            vmem((anc, anc), F32),
            vmem((block_rows, block_rows), BF16),
            vmem((block_rows, block_rows), BF16),
            vmem((block_rows, lead), BF16),
            vmem((block_rows, lead), BF16),
            vmem((anc, block_rows), BF16),
            vmem((anc, block_rows), BF16),
            vmem((anc, anc), BF16),
            vmem((anc, anc), BF16),
            vmem((block_rows, columns), F32),
            vmem((lead, columns), F32),
            vmem((count, anc, CHUNK), F32),
            vmem((owned, n_grid, anc, CHUNK), F32),
            vmem((owned, n_row, share, CHUNK), F32),
            vmem((owned, n_row, share, CHUNK), F32),
            vmem((owned, share, CHUNK), F32),
            vmem((owned, n_grid, share, CHUNK), F32),
            dma((6,)),
            dma((owned,)),
            dma((count // 2,)),
            dma((count,)),
            dma((count,)),
            dma((count,)),
            dma((owned, n_grid)),
            dma((owned, n_row)),
            dma((owned, n_row)),
            dma((owned, n_grid)),
            dma((owned, n_grid)),
        ],
        compiler_params=pltpu.CompilerParams(
            collective_id=0, has_side_effects=True, vmem_limit_bytes=56 * 1024 * 1024
        ),
        name="forward_solve",
    )(
        block_sizes, anc_rows.reshape(1, touched), leaf_rhs, leaf_lower, leaf_inverse, coupling,
        anc_rhs, anc_inverse,
    )


def solution(mesh):
    placed = (
        P(("grid", "row"), "rhs"),
        P(("grid", "row")),
        P(("grid", "row"), None),
        P(("grid", "row"), None),
        P(("grid", "row"), None),
        P(("grid", "row")),
        P(None, "rhs"),
        P(),
    )
    return jax.shard_map(
        body,
        mesh=mesh,
        in_specs=placed,
        out_specs=(P(("grid", "row"), "rhs"), P("row", "rhs")),
        check_vma=False,
    )
```
